128 devices in a mesh: dp: 8 (over y, z_hi), pipe: 2 (over z_lo), ts: 8 (over x, core).
Axes of the slice: x: 4, y: 4, z: 4 (z_hi: 2, z_lo: 2; z = z_hi * 2 + z_lo), core: 2. Of those that a mesh axis runs over, the one named last changes fastest.
Arguments:
- section_inputs: bfloat16 [8, 2, 1, 512, 4096], P('dp', 'pipe', None, 'ts'), may hold values from -6 to 6
- grad_out: bfloat16 [8, 1, 512, 4096], P('dp', None, 'ts'), may hold values from -6 to 6
- in_weight: bfloat16 [2, 4096, 6144], P('pipe', None, 'ts'), may hold values from -0.09375 to 0.09375
- out_weight: bfloat16 [2, 4096, 4096], P('pipe', 'ts'), may hold values from -0.09375 to 0.09375
- gains: bfloat16 [2, 4096], P('pipe'), may hold values from 0.5 to 1.5
- step_weight: bfloat16 [4096, 32], P(None, 'ts'), may hold values from -0.09375 to 0.09375
- decay_rate: float32 [32], P('ts'), may hold values from 0.01 to 1
Outputs:
- input_grads: bfloat16 [8, 2, 1, 512, 4096], P('dp', 'pipe', None, 'ts')
- in_weight_grad: float32 [2, 4096, 6144], P('pipe', 'dp', 'ts')
- out_weight_grad: float32 [2, 4096, 4096], P('pipe', 'ts', 'dp')
- gain_grad: float32 [2, 4096], P('pipe', ('dp', 'ts'))
- step_grad: float32 [4096, 32], P(('dp', 'pipe'), 'ts')
- rate_grad: float32 [32], P('ts')
The draws below stay inside these ranges and needn't reach their ends.
All inputs are finite; a program needn't handle non-finite values.
Results may differ from the reference program's by a relative error of at most 0.03.
Values may be sent and summed in bfloat16 or wider, within the bound.
A program may use at most 192 MiB of HBM per device.

```python
import math
import jax
import jax.numpy as jnp
from jax import lax

D = 4096
HD = 128
HEADS_DEV = 4
MB = 1
SEQ = 512
HEADS = 32
COLS = 6144
MIXW = 4096
REPLICAS = 8
N_PIPE = 2
N_TS = 8


def level_of(key, extent, shards, least, largest):
    factor_of = 1.0
    for dim, parts in shards:
        heights = jax.random.uniform(jax.random.fold_in(jax.random.fold_in(key, 6), dim), (parts,), jnp.float32, least / len(shards), largest / len(shards))
        factor_of = factor_of * jnp.repeat(jnp.exp(heights), extent[dim] // parts).reshape((-1,) + (1,) * (len(extent) - 1 - dim))
    return factor_of


def bell_draw(key, dims, deviation, limit, cuts=(), dtype=jnp.bfloat16):
    entries = deviation * jax.random.normal(key, dims, jnp.float32)
    if cuts:
        entries = entries * level_of(key, dims, cuts, -0.22, 0.18)
    return jnp.clip(entries, -limit, limit).astype(dtype)


def setup_inputs(seed: int = 0) -> dict:
    seeds = jax.random.split(jax.random.key(seed), 8)
    section_inputs = bell_draw(seeds[0], (REPLICAS, N_PIPE, MB, SEQ, D), 1.0, 6.0, ((0, 8), (1, 2), (3, 8)))
    grad_out = bell_draw(seeds[1], (REPLICAS, MB, SEQ, D), 1.0, 6.0, ((0, 8), (2, 8)))
    in_weight = bell_draw(seeds[2], (N_PIPE, D, COLS), D ** -0.5, 0.09375, ((0, 2), (2, 8)))
    out_weight = bell_draw(seeds[3], (N_PIPE, MIXW, D), MIXW ** -0.5, 0.09375, ((0, 2), (1, 8)))
    gains = jnp.clip(1.0 + 0.1 * jax.random.normal(seeds[4], (N_PIPE, D), jnp.float32), 0.5, 1.5).astype(jnp.bfloat16)
    step_weight = bell_draw(seeds[5], (D, HEADS), D ** -0.5, 0.09375, ((1, 8),))
    decay_rate = jnp.clip(jnp.exp(math.log(1.0) - 4.6051702 * jax.random.uniform(seeds[6], (HEADS,), jnp.float32) ** level_of(seeds[6], (HEADS,), ((0, 8),), -0.2, 0.2)), 0.01, 1.0)
    return dict(section_inputs=section_inputs, grad_out=grad_out, in_weight=in_weight, out_weight=out_weight, gains=gains, step_weight=step_weight, decay_rate=decay_rate)


highest = lax.Precision.HIGHEST

def normed(features, scales):
    return features * lax.rsqrt(lax.optimization_barrier(jnp.mean(features * features, axis=-1, keepdims=True)) + 1e-05) * scales

def attend(projected, logits, decay_rates):
    length = projected.shape[0]
    head_count = decay_rates.shape[0]
    head_width = projected.shape[1] // (head_count + 2)
    queries = projected[:, :head_count * head_width].reshape(length, head_count, head_width)
    keys_part = projected[:, head_count * head_width:(head_count + 1) * head_width]
    values_part = projected[:, (head_count + 1) * head_width:]
    scores = jnp.einsum('shd,td->hst', queries, keys_part, precision=highest) * head_width ** (-0.5)
    causal = jnp.arange(length)[:, None] >= jnp.arange(length)[None, :]
    scores = jnp.where(causal[None], scores, -1e+30)
    weights = jax.nn.softmax(scores, axis=-1)
    mixed_out = jnp.einsum('hst,td->shd', weights, values_part, precision=highest)
    return mixed_out.reshape(length, head_count * head_width)

def selective(projected, logits, decay_rates):
    length = projected.shape[0]
    head_count = decay_rates.shape[0]
    head_width = projected.shape[1] // (head_count + 2)
    inputs_part = projected[:, :head_count * head_width].reshape(length, head_count, head_width)
    write_part = projected[:, head_count * head_width:(head_count + 1) * head_width]
    read_part = projected[:, (head_count + 1) * head_width:]
    step_sizes = jax.nn.softplus(logits)
    totals = jnp.cumsum(-step_sizes * decay_rates[None, :], axis=0)
    causal = jnp.arange(length)[:, None] >= jnp.arange(length)[None, :]
    log_gaps = jnp.where(causal[:, :, None], totals[:, None, :] - totals[None, :, :], -1e+30)
    decays = jnp.exp(log_gaps)
    intersection = jnp.dot(read_part, write_part.T, precision=highest) * head_width ** (-0.5)
    mixing = decays * intersection[:, :, None] * step_sizes[None, :, :]
    mixed_out = jnp.einsum('sth,thd->shd', mixing, inputs_part, precision=highest)
    return mixed_out.reshape(length, head_count * head_width)

def section_backward(section_in, cotangent, in_w, out_w, gain, step_w, decay_rates, section_index):
    groups = N_TS
    length = section_in.shape[0]
    block_width = (HEADS_DEV + 2) * HD
    mix_width = HEADS_DEV * HD
    inputs_wide = section_in.astype(jnp.float32)
    gain_wide = gain.astype(jnp.float32)
    normal = normed(inputs_wide, gain_wide).astype(jnp.bfloat16)
    projected = jnp.dot(normal, in_w, preferred_element_type=jnp.float32).astype(jnp.bfloat16)
    logits = jnp.dot(normal, step_w, preferred_element_type=jnp.float32)
    mixer_fn = attend if section_index == 0 else selective

    def grouped(proj_wide, logit_wide, rate_wide):
        pieces = proj_wide.reshape(length, groups, block_width).transpose(1, 0, 2)
        logit_pieces = logit_wide.reshape(length, groups, HEADS_DEV).transpose(1, 0, 2)
        rate_pieces = rate_wide.reshape(groups, HEADS_DEV)
        outputs = jax.vmap(mixer_fn)(pieces, logit_pieces, rate_pieces)
        return outputs.transpose(1, 0, 2).reshape(length, groups * mix_width)
    mixed_wide, backward = jax.vjp(grouped, projected.astype(jnp.float32), logits, decay_rates)
    mixed = mixed_wide.astype(jnp.bfloat16)
    mix_grad = jnp.dot(cotangent, out_w.T, preferred_element_type=jnp.float32).astype(jnp.bfloat16)
    proj_grad_wide, logit_grad, rates_grad = backward(mix_grad.astype(jnp.float32))
    proj_grad = proj_grad_wide.astype(jnp.bfloat16)
    partial_terms = jnp.einsum('sgc,dgc->gsd', proj_grad.astype(jnp.float32).reshape(length, groups, block_width), in_w.astype(jnp.float32).reshape(-1, groups, block_width), precision=highest)
    partial_terms = partial_terms + jnp.einsum('sgh,dgh->gsd', logit_grad.reshape(length, groups, HEADS_DEV), step_w.astype(jnp.float32).reshape(-1, groups, HEADS_DEV), precision=highest)
    normal_grad = lax.optimization_barrier(jnp.sum(lax.optimization_barrier(partial_terms.astype(jnp.bfloat16)).astype(jnp.float32), axis=0))
    unused_out, norm_back = jax.vjp(normed, inputs_wide, gain_wide)
    input_grad, gain_term = norm_back(normal_grad)
    section_grad = (cotangent.astype(jnp.float32) + input_grad).astype(jnp.bfloat16)
    in_term = jnp.dot(normal.T, proj_grad, preferred_element_type=jnp.float32)
    out_term = jnp.dot(mixed.T, cotangent, preferred_element_type=jnp.float32)
    step_term = jnp.dot(normal.astype(jnp.float32).T, logit_grad, precision=highest)
    return (section_grad, in_term, out_term, gain_term, step_term, rates_grad)

def rounded(array_wide):
    return lax.optimization_barrier(array_wide.astype(jnp.bfloat16)).astype(jnp.float32)

def reference(section_inputs, grad_out, in_weight, out_weight, gains, step_weight, decay_rate):

    def replica(running, replica_data):
        inputs_rep, cotangents = replica_data
        in_total, out_total, gain_total, step_total, rate_total = running
        in_parts = [jnp.zeros(in_weight.shape[1:], jnp.float32) for section_index in range(2)]
        out_parts = [jnp.zeros(out_weight.shape[1:], jnp.float32) for section_index in range(2)]
        gain_parts = [jnp.zeros(gains.shape[1:], jnp.float32) for section_index in range(2)]
        earlier_grads = []
        later_grads = []
        for micro_index in range(MB):
            later = section_backward(inputs_rep[1, micro_index], cotangents[micro_index], in_weight[1], out_weight[1], gains[1], step_weight, decay_rate, 1)
            earlier = section_backward(inputs_rep[0, micro_index], later[0], in_weight[0], out_weight[0], gains[0], step_weight, decay_rate, 0)
            later_grads.append(later[0])
            earlier_grads.append(earlier[0])
            in_parts = [in_parts[0] + earlier[1], in_parts[1] + later[1]]
            out_parts = [out_parts[0] + earlier[2], out_parts[1] + later[2]]
            gain_parts = [gain_parts[0] + earlier[3], gain_parts[1] + later[3]]
            step_total = step_total + later[4] + earlier[4]
            rate_total = rate_total + later[5] + earlier[5]
        in_total = in_total + rounded(jnp.stack(in_parts))
        out_total = out_total + rounded(jnp.stack(out_parts))
        gain_total = gain_total + jnp.stack(gain_parts)
        section_grads = jnp.stack([jnp.stack(earlier_grads), jnp.stack(later_grads)])
        return ((in_total, out_total, gain_total, step_total, rate_total), section_grads)
    initial = (jnp.zeros(in_weight.shape, jnp.float32), jnp.zeros(out_weight.shape, jnp.float32), jnp.zeros(gains.shape, jnp.float32), jnp.zeros(step_weight.shape, jnp.float32), jnp.zeros(decay_rate.shape, jnp.float32))
    finals, input_grads = lax.scan(replica, initial, (section_inputs, grad_out))
    return (input_grads, finals[0], finals[1], finals[2], finals[3], finals[4])
```

```python
import jax
import jax.numpy as jnp
from jax import lax
from jax.experimental import pallas as pl
from jax.experimental.pallas import tpu as pltpu
from jax.sharding import PartitionSpec as P

F32 = jnp.float32
BF16 = jnp.bfloat16
HIGHEST = lax.Precision.HIGHEST
D = 4096
SEQ = 512
HD = 128
HEADS = 4
BW = 768
MW = 512
CH = 4
HS = 16
OWN = 64
AUX = 16
SCALE = HD**-0.5
HALF = D // 2


def mm(a, b, **kw):
    return lax.dot_general(a, b, (((1,), (0,)), ((), ())), preferred_element_type=F32, **kw)


def mm_nt(a, b, **kw):
    return lax.dot_general(a, b, (((1,), (1,)), ((), ())), preferred_element_type=F32, **kw)


def mm_tn(a, b, **kw):
    return lax.dot_general(a, b, (((0,), (0,)), ((), ())), preferred_element_type=F32, **kw)


def aligned(value, by):
    return pl.multiple_of(value, by)


def kernel(
    x_ref, go_hbm, inw_hbm, outw_hbm, gain_ref, step_ref, rate_ref,
    ig_ref, ing_ref, outg_ref, gaing_ref, aux_ref,
    nall, up, inw, outw, proj, projg, mixg, mixed, pbuf, xd, lrow, lcol, dtb, lgb, dl, acc,
    pgc, terms, xsib, rl, rb, nd, dd, ma, pa, sm, gacc, gx, auxr, swt_ref,
    lsem, ssem, rsem,
):
    d = lax.axis_index("dp")
    p = lax.axis_index("pipe")
    t = lax.axis_index("ts")
    x, c = t // 2, t % 2
    y, z = d // 2, d % 2
    xr, xl, x2 = (x + 1) % 4, (x + 3) % 4, (x + 2) % 4
    yu, yd, y2 = (y + 1) % 4, (y + 3) % 4, (y + 2) % 4
    right, left, far, sib = (d, p, xr * 2 + c), (d, p, xl * 2 + c), (d, p, x2 * 2 + c), (d, p, x * 2 + 1 - c)
    other = (d, 1 - p, t)
    upper, lower, zpar = (yu * 2 + z, p, t), (yd * 2 + z, p, t), (y * 2 + 1 - z, p, t)
    yfar = (y2 * 2 + z, p, t)
    peers = {(i, j): (((y + i) % 4) * 2 + (z + j) % 2, p, t) for i in range(4) for j in range(2) if i or j}

    names = {}

    def rc(name, src, dst, dev):
        k = names.setdefault(name, len(names))
        return pltpu.make_async_remote_copy(
            src, dst, ssem.at[k], rsem.at[k], device_id=dev, device_id_type=pl.DeviceIdType.MESH
        )

    def base(xx, cc, off=0):
        return aligned((xx * 2 + cc) * OWN + off, HS)

    cp_in = pltpu.make_async_copy(inw_hbm, inw, lsem.at[0])
    cp_out = pltpu.make_async_copy(outw_hbm, outw, lsem.at[1])
    cp_go = pltpu.make_async_copy(go_hbm, up.at[pl.ds(base(x, c), OWN)], lsem.at[2])
    cp_in.start()
    cp_out.start()

    @pl.when(p == 1)
    def _():
        cp_go.start()

    bar = pltpu.get_barrier_semaphore()
    partners = (right, left, far, sib, other) + tuple(peers.values())
    for dev in partners:
        pl.semaphore_signal(bar, inc=1, device_id=dev, device_id_type=pl.DeviceIdType.MESH)

    xw = x_ref[...].astype(F32)
    gw = gain_ref[...].astype(F32)
    rinv = lax.rsqrt(jnp.mean(xw * xw, axis=-1, keepdims=True) + 1e-05)
    nall[pl.ds(base(x, c), OWN)] = (xw * rinv * gw).astype(BF16)
    pl.semaphore_wait(bar, len(partners))

    def gather(key, buf, off, n, stacked=False):
        def part(xx, half=None, cc=c):
            rows = pl.ds(base(xx, cc, off), n)
            if stacked:
                return buf.at[pl.ds((half or 0) * 4, 8 if half is None else 4), rows]
            if half is None:
                return buf.at[rows]
            return buf.at[rows, pl.ds(half * HALF, HALF)]

        def move(k, ref, dev):
            return rc((key, k), ref, ref, dev)

        g = dict(
            ra=move("ra", part(x, 0), right), lb=move("lb", part(x, 1), left), s=move("s", part(x), sib),
            rb=move("rb", part(x, 1), right), la=move("la", part(x, 0), left),
            fr=move("fr", part(xl, 0), right), fl=move("fl", part(xr, 1), left),
            s1=move("s1", part(xl), sib), s2=move("s2", part(xr), sib), s3=move("s3", part(x2), sib),
        )

        def start():
            for k in ("ra", "lb", "s", "rb", "la"):
                g[k].start()

        def mid():
            g["ra"].wait_recv()
            g["fr"].start()
            g["lb"].wait_recv()
            g["fl"].start()
            g["rb"].wait_recv()
            g["s1"].start()
            g["la"].wait_recv()
            g["s2"].start()

        def end():
            g["fr"].wait_recv()
            g["fl"].wait_recv()
            g["s3"].start()
            for k in ("s", "s1", "s2", "s3"):
                g[k].wait_recv()

        def sent():
            for k in g:
                g[k].wait_send()

        return start, mid, end, sent

    n_start, n_mid, n_end, n_sent = gather("n", nall, 0, OWN)
    n_start()

    def spread(key, buf, dst):
        mine = pl.ds(base(x, c), OWN)
        copies = [
            rc((key, rel), buf.at[mine, pl.ds(aligned(dev[0] * 512, 512), 512)], dst.at[d, mine], dev)
            for rel, dev in peers.items()
        ]

        def start():
            for copy in copies:
                copy.start()
            dst[d, mine] = buf[mine, pl.ds(aligned(d * 512, 512), 512)]

        def arrive():
            for copy in copies:
                copy.wait_recv()

        def sent():
            for copy in copies:
                copy.wait_send()

        return start, arrive, sent

    ns_start, ns_arrive, ns_sent = spread("ns", nall, nd)
    ds_start, ds_arrive, ds_sent = spread("ds", up, dd)
    nx_start, nx_mid, nx_end, nx_sent = gather("nx", nd, 0, OWN, True)
    dx_start, dx_mid, dx_end, dx_sent = gather("dx", dd, 0, OWN, True)
    ns_start()
    swt_ref[...] = jnp.zeros_like(swt_ref)
    swt_ref[0:HEADS] = step_ref[...]
    n_mid()

    @pl.when(p == 1)
    def _():
        u_start, _m, _e, _s = gather("u", up, 0, OWN)
        cp_go.wait()
        u_start()
        ds_start()

    n_end()
    cp_in.wait()

    @pl.loop(0, 2)
    def _(i):
        rows = pl.ds(aligned(i * 256, 256), 256)
        proj[rows] = mm(nall[rows], inw[...]).astype(BF16)

    def causal(tb):
        r = lax.broadcasted_iota(jnp.int32, (HD, SEQ), 0) + tb * HD
        return r >= lax.broadcasted_iota(jnp.int32, (HD, SEQ), 1)

    def hc(h):
        return slice(h * HD, (h + 1) * HD)

    def mix_gradient():
        @pl.loop(0, 2)
        def _(i):
            rows = pl.ds(aligned(i * 256, 256), 256)
            mixg[rows] = mm_nt(up[rows], outw[...]).astype(BF16)

    lane = lax.broadcasted_iota(jnp.int32, (SEQ, HD), 1)

    def rates_row():
        one = lax.broadcasted_iota(jnp.int32, (1, HD), 1)
        row = jnp.zeros((1, HD), F32)
        for h in range(HEADS):
            row = jnp.where(one == h, rate_ref[h], row)
        return row

    def ssm_steps():
        lg = mm_nt(nall[...], swt_ref[...])
        lgb[...] = jnp.zeros_like(lgb)
        lgb[:, 0:AUX] = lg
        lgw = lgb[...]
        dt = jnp.maximum(lgw, 0.0) + jnp.log1p(jnp.exp(-jnp.abs(lgw)))
        dtb[...] = dt
        steps = -dt * rates_row()
        tril = (
            lax.broadcasted_iota(jnp.int32, (SEQ, SEQ), 0) >= lax.broadcasted_iota(jnp.int32, (SEQ, SEQ), 1)
        ).astype(F32)
        totals = mm(tril, steps, precision=HIGHEST)
        lcol[...] = totals
        lrow[...] = totals.T
        for h in range(HEADS):
            xd[:, hc(h)] = (proj[:, hc(h)].astype(F32) * dt[:, h : h + 1]).astype(BF16)

    def ssm_forward():
        @pl.loop(0, 4)
        def _(tb):
            rows = pl.ds(aligned(tb * HD, HD), HD)
            inter = mm_nt(proj[rows, 640:768], proj[:, 512:640]) * SCALE
            mask = causal(tb)
            lc = lcol[rows]
            for h in range(HEADS):
                e = jnp.exp(jnp.where(mask, lc[:, h : h + 1] - lrow[h : h + 1, :], -1e30))
                m = (e * inter).astype(BF16)
                pbuf[h, rows] = m
                mixed[rows, hc(h)] = mm(m, xd[:, hc(h)]).astype(BF16)

    def ssm_backward():
        small_lane = lax.broadcasted_iota(jnp.int32, (HD, HD), 1)

        for tb in range(4):
            rows, w = slice(tb * HD, (tb + 1) * HD), (tb + 1) * HD
            mask = causal(tb)[:, 0:w]
            lc = lcol[rows]
            ds = jnp.zeros((HD, w), F32)
            sums = jnp.zeros((HD, HD), F32)
            for h in range(HEADS):
                dm = mm_nt(mixg[rows, hc(h)], xd[0:w, hc(h)])
                e = jnp.exp(jnp.where(mask, lc[:, h : h + 1] - lrow[h : h + 1, 0:w], -1e30))
                ds = ds + dm * e
                row_sum = jnp.sum(dm * pbuf[h, rows, 0:w].astype(F32), axis=-1, keepdims=True)
                sums = jnp.where(small_lane == h, row_sum, sums)
            dl[rows] = sums
            dsb = (ds * SCALE).astype(BF16)
            projg[rows, 640:768] = mm(dsb, proj[0:w, 512:640]).astype(BF16)
            contrib = mm_tn(dsb, proj[rows, 640:768])
            if tb:
                acc[0, 0 : w - HD] = acc[0, 0 : w - HD] + contrib[0 : w - HD]
            acc[0, w - HD : w] = contrib[w - HD :]

        projg[:, 512:640] = acc[0].astype(BF16)
        dt = dtb[...]
        dlv = dl[...]
        cpv = jnp.zeros((SEQ, HD), F32)
        for h in range(HEADS):
            dxp = jnp.concatenate(
                [mm_tn(pbuf[h, sb:, sb : sb + HD], mixg[sb:, hc(h)]) for sb in range(0, SEQ, HD)], axis=0
            )
            projg[:, hc(h)] = (dxp * dt[:, h : h + 1]).astype(BF16)
            col = jnp.sum(dxp * xd[:, hc(h)].astype(F32), axis=-1, keepdims=True)
            colp = jnp.sum(dxp * proj[:, hc(h)].astype(F32), axis=-1, keepdims=True)
            dlv = jnp.where(lane == h, dlv - col, dlv)
            cpv = jnp.where(lane == h, colp, cpv)
        triu = (
            lax.broadcasted_iota(jnp.int32, (SEQ, SEQ), 0) <= lax.broadcasted_iota(jnp.int32, (SEQ, SEQ), 1)
        ).astype(F32)
        rev = mm(triu, dlv, precision=HIGHEST)
        lgg = (cpv - rates_row() * rev) * jax.nn.sigmoid(lgb[...])
        lgg = jnp.where(lane < HEADS, lgg, 0.0)
        projg[:, 768:896] = lgg.astype(BF16)
        sm[d, :, 0:SEQ] = lgg.T[0:AUX, :].astype(BF16)
        rates = -jnp.sum(dt * rev, axis=0, keepdims=True)
        sm[d, :, SEQ:] = jnp.broadcast_to(rates, (AUX, HD)).astype(BF16)

    def attn_forward():
        @pl.loop(0, 4)
        def _(tb):
            rows = pl.ds(aligned(tb * HD, HD), HD)
            mask = causal(tb)
            for h in range(HEADS):
                s = jnp.where(mask, mm_nt(proj[rows, hc(h)], proj[:, 512:640]) * SCALE, -1e30)
                e = jnp.exp(s - jnp.max(s, axis=-1, keepdims=True))
                w = (e / jnp.sum(e, axis=-1, keepdims=True)).astype(BF16)
                pbuf[h, rows] = w
                mixed[rows, hc(h)] = mm(w, proj[:, 640:768]).astype(BF16)

    def attn_backward():
        for tb in range(4):
            rows, w = slice(tb * HD, (tb + 1) * HD), (tb + 1) * HD
            ds_all, q_all, w_all, g_all = [], [], [], []
            for h in range(HEADS):
                gb = mixg[rows, hc(h)]
                wb = pbuf[h, rows, 0:w]
                ww = wb.astype(F32)
                dw = mm_nt(gb, proj[0:w, 640:768])
                ds = (ww * (dw - jnp.sum(ww * dw, axis=-1, keepdims=True)) * SCALE).astype(BF16)
                projg[rows, hc(h)] = mm(ds, proj[0:w, 512:640]).astype(BF16)
                ds_all.append(ds)
                w_all.append(wb)
                g_all.append(gb)
                q_all.append(proj[rows, hc(h)])
            dk = mm_tn(jnp.concatenate(ds_all, axis=0), jnp.concatenate(q_all, axis=0))
            dv = mm_tn(jnp.concatenate(w_all, axis=0), jnp.concatenate(g_all, axis=0))
            if tb:
                acc[0, 0 : w - HD] = acc[0, 0 : w - HD] + dk[0 : w - HD]
                acc[1, 0 : w - HD] = acc[1, 0 : w - HD] + dv[0 : w - HD]
            acc[0, w - HD : w] = dk[w - HD :]
            acc[1, w - HD : w] = dv[w - HD :]
        projg[:, 512:640] = acc[0].astype(BF16)
        projg[:, 640:768] = acc[1].astype(BF16)
        projg[:, 768:896] = jnp.zeros((SEQ, HD), BF16)

    def scatter_terms(after_chunk, beside):
        for h in range(CH):
            for cc in range(2):
                for xx in range(4):
                    src = (xx * 2 + cc) * OWN + h * HS
                    dst = (cc * 4 + xx) * HS
                    pgc[h, dst : dst + HS] = projg[src : src + HS]

        def rows_of(h, xx, half=None):
            rows = pl.ds(aligned(xx * HS, HS), HS)
            if half is None:
                return terms.at[h, c, rows]
            return terms.at[h, c, rows, pl.ds(half * HALF, HALF)]

        def copies(h):
            return dict(
                sib=rc(("x", h, "sib"), terms.at[h, 1 - c], xsib.at[h], sib),
                r1=rc(("x", h, "r1"), rows_of(h, x2, 0), rl.at[h, 0], right),
                l1=rc(("x", h, "l1"), rows_of(h, x2, 1), rl.at[h, 1], left),
                r2=rc(("x", h, "r2"), rows_of(h, xr, 1), rb.at[h, 0, :, pl.ds(HALF, HALF)], right),
                l2=rc(("x", h, "l2"), rows_of(h, xl, 0), rb.at[h, 1, :, pl.ds(0, HALF)], left),
                r3=rc(("x", h, "r3"), rows_of(h, xr, 0), rb.at[h, 0, :, pl.ds(0, HALF)], right),
                l3=rc(("x", h, "l3"), rows_of(h, xl, 1), rb.at[h, 1, :, pl.ds(HALF, HALF)], left),
            )

        cs = [copies(h) for h in range(CH)]

        def stage_a(h):
            lhs = pgc[h : h + 2].reshape(16 * HS, BW + HD)

            @pl.loop(0, 4)
            def _(n):
                cols = pl.ds(aligned(n * 1024, 1024), 1024)
                val = mm_nt(lhs[:, 0:BW], inw[cols, :]) + mm(lhs[:, BW : BW + AUX], swt_ref[:, cols])
                val = val.astype(BF16)
                for i in range(4):
                    terms[h + i // 2, i % 2, :, cols] = val[i * 64 : (i + 1) * 64]

            cs[h]["sib"].start()
            cs[h + 1]["sib"].start()

        def stage_b(h):
            cs[h]["sib"].wait_recv()

            @pl.loop(0, 4)
            def _(i):
                rows = pl.ds(aligned(i * HS, HS), HS)
                terms[h, c, rows] = (terms[h, c, rows].astype(F32) + xsib[h, rows].astype(F32)).astype(BF16)

            cs[h]["r1"].start()
            cs[h]["l1"].start()

        def stage_e(h):
            cs[h]["r2"].start()
            cs[h]["l2"].start()

        def stage_c(h):
            cs[h]["r1"].wait_recv()
            rows, cols = pl.ds(aligned(xr * HS, HS), HS), pl.ds(0, HALF)
            terms[h, c, rows, cols] = (terms[h, c, rows, cols].astype(F32) + rl[h, 0].astype(F32)).astype(BF16)
            cs[h]["r3"].start()
            cs[h]["l1"].wait_recv()
            rows, cols = pl.ds(aligned(xl * HS, HS), HS), pl.ds(HALF, HALF)
            terms[h, c, rows, cols] = (terms[h, c, rows, cols].astype(F32) + rl[h, 1].astype(F32)).astype(BF16)
            cs[h]["l3"].start()

        def stage_d(h):
            for k in ("r2", "l2", "r3", "l3"):
                cs[h][k].wait_recv()
            rows = pl.ds(aligned(x * HS, HS), HS)
            ng = terms[h, c, rows].astype(F32) + rb[h, 0].astype(F32) + rb[h, 1].astype(F32)
            mine = slice(h * HS, (h + 1) * HS)
            xv = x_ref[mine].astype(F32)
            r = lax.rsqrt(jnp.mean(xv * xv, axis=-1, keepdims=True) + 1e-05)
            term = jnp.sum(xv * r * ng, axis=0, keepdims=True)
            for i in range(8):
                part = term[:, i * 512 : (i + 1) * 512]
                gacc[0, i : i + 1] = part if h == 0 else gacc[0, i : i + 1] + part
            ngg = ng * gain_ref[...].astype(F32)
            dot = jnp.mean(xv * ngg, axis=-1, keepdims=True)
            dy = up[pl.ds(base(x, c, h * HS), HS)].astype(F32)
            ig_ref[mine] = (dy + r * ngg - xv * (r * r * r * dot)).astype(BF16)
            after_chunk(h)

        plan = ("a0", "b0", "e0", "b1", "a2", "c0", "e1", "b2", "c1", "d0", "e2", "b3", "c2", "d1", "e3", "c3", "d2", "d3")
        stages = dict(a=stage_a, b=stage_b, c=stage_c, d=stage_d, e=stage_e)
        for i, step in enumerate(plan):
            stages[step[0]](int(step[1]))
            for extra in beside.get(step, ()):
                extra()
        for h in range(CH):
            for k in cs[h]:
                cs[h][k].wait_send()

    def handed(h):
        rows = pl.ds(base(x, c, h * HS), HS)
        return rc(("z", h), ig_ref.at[pl.ds(h * HS, HS)], up.at[rows], other)

    class Spread:
        def __init__(self, key, buf):
            first, rest = pl.ds(0, NA), pl.ds(NA, SEQ - NA)
            hb = (SEQ - NA) // 2
            low, high = pl.ds(NA, hb), pl.ds(NA + hb, hb)
            self.all = []

            def move(name, yy, zz, rows, dev):
                ref = buf.at[yy * 2 + zz, rows]
                copy = rc((key, name), ref, ref, dev)
                self.all.append(copy)
                return copy

            self.za = move("za", y, z, first, zpar)
            self.ua, self.da = move("ua", y, z, first, upper), move("da", y, z, first, lower)
            self.up, self.dp = move("up", y, 1 - z, first, upper), move("dp", y, 1 - z, first, lower)
            self.ur, self.dr = move("ur", yd, z, first, upper), move("dr", yu, 1 - z, first, lower)
            self.ub, self.db = move("ub", y, z, rest, upper), move("db", y, z, rest, lower)
            self.ubr, self.dbr = move("ubr", yd, z, low, upper), move("dbr", yu, z, high, lower)
            self.zb = [move(("zb", k), yy, z, rest, zpar) for k, yy in enumerate((y, yd, yu, y2))]

        def start(self):
            for copy in (self.za, self.ub, self.db, self.ua, self.da, self.zb[0]):
                copy.start()

        def s1(self):
            self.ub.wait_recv()
            self.ubr.start()
            self.zb[1].start()
            self.db.wait_recv()
            self.dbr.start()
            self.zb[2].start()

        def s2(self):
            self.za.wait_recv()
            self.up.start()
            self.dp.start()

        def s3(self):
            self.ubr.wait_recv()
            self.dbr.wait_recv()
            self.zb[3].start()

        def s4(self):
            self.ua.wait_recv()
            self.ur.start()

        def s5(self):
            self.da.wait_recv()
            self.up.wait_recv()
            self.dp.wait_recv()
            self.dr.start()

        def end(self, use=lambda yy, zz: None):
            self.zb[0].wait_recv()
            use(y, 1 - z)
            self.zb[1].wait_recv()
            use(yd, 1 - z)
            self.zb[2].wait_recv()
            use(yu, 1 - z)
            self.ur.wait_recv()
            use(y2, z)
            self.zb[3].wait_recv()
            self.dr.wait_recv()
            use(y2, 1 - z)

        def sent(self):
            for copy in self.all:
                copy.wait_send()

    mix_all, grad_all = Spread("m", ma), Spread("p", pa)

    def mix_start():
        ma[d] = mixed[...]
        mix_all.start()

    def grad_start():
        pa[d] = projg[:, 0:BW]
        grad_all.start()

    def out_sum():
        outg_ref[...] = mm_tn(ma[0], dd[0])

        @pl.loop(1, 8)
        def _(r):
            outg_ref[...] = outg_ref[...] + mm_tn(ma[r], dd[r])

    def in_first():
        ing_ref[...] = mm_tn(nd[d], pa[d])

    def in_add(yy, zz):
        k = yy * 2 + zz
        ing_ref[...] = ing_ref[...] + mm_tn(nd[k], pa[k])

    sms = [rc(("sm", rel), sm.at[d], sm.at[d], dev) for rel, dev in peers.items()]
    rec = rc("rec", aux_ref, auxr, other)

    def small_start():
        for copy in sms:
            copy.start()

    def small_end():
        for copy in sms:
            copy.wait_recv()
        steps = jnp.zeros((AUX, 512), F32)
        rates = jnp.zeros((AUX, HD), F32)
        for r in range(8):
            steps = steps + mm(sm[r, :, 0:SEQ], nd[r])
            rates = rates + sm[r, :, SEQ:].astype(F32)
        aux_ref[...] = jnp.zeros_like(aux_ref)
        aux_ref[:, 0:512] = steps
        aux_ref[:, 512:640] = rates
        rec.start()

    def gmove(name, a, b, dev):
        return rc(("gain", name), gacc.at[a], gx.at[b], dev)

    g_core = [gmove("c", 0, 0, sib)]
    g_x = [gmove("x0", 1, 1, right), gmove("x1", 1, 2, left), gmove("x2", 1, 3, far)]
    g_y = [gmove("y0", 2, 4, upper), gmove("y1", 2, 5, lower), gmove("y2", 2, 6, yfar)]
    g_z = [gmove("z", 3, 7, zpar)]

    def gain_start(group):
        for copy in group:
            copy.start()

    def gain_add(group, at, slots):
        for copy in group:
            copy.wait_recv()
        total = gacc[at]
        for k in slots:
            total = total + gx[k]
        gacc[at + 1] = total

    def gain_1():
        gain_start(g_core)

    def gain_2():
        gain_add(g_core, 0, (0,))
        gain_start(g_x)

    def gain_3():
        gain_add(g_x, 1, (1, 2, 3))
        gain_start(g_y)

    def gain_4():
        gain_add(g_y, 2, (4, 5, 6))
        gain_start(g_z)

    def gain_5():
        gain_add(g_z, 3, (7,))
        whole = gacc[4]
        mine = jnp.where(lax.broadcasted_iota(jnp.int32, (8, 512), 0) == d, whole, 0.0)
        pick = (
            lax.broadcasted_iota(jnp.int32, (512, 64), 0) == lax.broadcasted_iota(jnp.int32, (512, 64), 1) + t * 64
        ).astype(F32)
        gaing_ref[...] = jnp.sum(mm(mine, pick, precision=HIGHEST), axis=0, keepdims=True)
        for copy in g_core + g_x + g_y + g_z:
            copy.wait_send()

    @pl.when(p == 1)
    def _():
        ssm_steps()
        _st, u_mid, u_end, u_sent = gather("u", up, 0, OWN)
        u_mid()
        ssm_forward()
        ns_arrive()
        nx_start()
        mix_start()
        u_end()
        cp_out.wait()
        mix_gradient()
        ssm_backward()
        nx_mid()
        small_start()
        scatter_terms(lambda h: handed(h).start(), {})
        grad_start()
        nx_end()
        gain_1()
        ds_arrive()
        dx_start()
        mix_all.s1()
        mix_all.s2()
        gain_2()
        grad_all.s1()
        mix_all.s3()
        gain_3()
        mix_all.s4()
        mix_all.s5()
        grad_all.s2()
        dx_mid()
        gain_4()
        grad_all.s3()
        grad_all.s4()
        grad_all.s5()
        gain_5()
        dx_end()
        small_end()
        mix_all.end()
        out_sum()
        in_first()
        in_add(yu, z)
        in_add(yd, z)
        grad_all.end(in_add)
        u_sent()
        for h in range(CH):
            handed(h).wait_send()
        for copy in sms:
            copy.wait_send()
        rec.wait_send()

    @pl.when(p == 0)
    def _():
        attn_forward()
        ns_arrive()
        nx_start()
        mix_start()
        mix_all.s1()
        mix_all.s2()
        nx_mid()
        mix_all.s3()
        mix_all.s4()
        mix_all.s5()
        nx_end()
        gs = [gather(("e", h), up, h * HS, HS) for h in range(CH)]

        def arrive(h):
            handed(h).wait_recv()
            gs[h][0]()

        arrive(0)
        for h in range(1, CH):
            arrive(h)
            gs[h - 1][1]()
            if h >= 2:
                gs[h - 2][2]()
        ds_start()
        gs[CH - 1][1]()
        gs[CH - 2][2]()
        gs[CH - 1][2]()
        cp_out.wait()
        mix_gradient()
        ds_arrive()
        dx_start()
        attn_backward()
        grad_start()
        in_first()
        mix_all.end()
        scatter_terms(
            lambda h: None,
            {
                "a0": [dx_mid],
                "b1": [grad_all.s1, grad_all.s2],
                "a2": [dx_end],
                "c1": [out_sum],
                "d0": [grad_all.s3],
                "d1": [grad_all.s4],
            },
        )
        gain_1()
        grad_all.s5()
        gain_2()
        in_add(yu, z)
        gain_3()
        in_add(yd, z)
        gain_4()
        gain_5()
        grad_all.end(in_add)
        for h in range(CH):
            gs[h][3]()
        rec.wait_recv()
        aux_ref[...] = auxr[...]

    n_sent()
    ns_sent()
    ds_sent()
    nx_sent()
    dx_sent()
    mix_all.sent()
    grad_all.sent()


NA = 288

N_SEMS = 240


def finish(ig_in, ing_in, outg_in, gaing_in, aux_in, ig, ing, outg, gaing, step, rates, b0, b1, b2, sems):
    ins, outs = [], []
    for src, mid, dst in ((ing_in, b1, ing), (outg_in, b2, outg), (ig_in, b0, ig)):
        n = src.shape[0] // 4
        for i in range(4):
            rows, k = pl.ds(i * n, n), len(ins)
            ins.append(pltpu.make_async_copy(src.at[rows], mid.at[rows], sems.at[0, k]))
            outs.append(pltpu.make_async_copy(mid.at[rows], dst.at[rows], sems.at[1, k]))
    for copy in ins:
        copy.start()
    for k in range(len(ins)):
        ins[k].wait()
        outs[k].start()
    gaing[...] = gaing_in[...]
    p = lax.axis_index("pipe")
    rows = jnp.where(p == 0, aux_in[:, 0:256], aux_in[:, 256:512])
    step[...] = rows[0:HEADS]
    rates[...] = aux_in[0:1, 512 : 512 + HEADS]
    for copy in outs:
        copy.wait()


def shards(section_inputs, grad_out, in_weight, out_weight, gains, step_weight, decay_rate):
    vm = pl.BlockSpec(memory_space=pltpu.VMEM)
    hbm = pl.BlockSpec(memory_space=pl.ANY)
    v = pltpu.VMEM
    far = pl.BlockSpec(memory_space=pltpu.HBM)
    ig, ing, outg, gaing, aux = pl.pallas_call(
        kernel,
        out_shape=(
            jax.ShapeDtypeStruct((OWN, D), BF16),
            jax.ShapeDtypeStruct((512, BW), F32),
            jax.ShapeDtypeStruct((MW, 512), F32),
            jax.ShapeDtypeStruct((1, 64), F32),
            jax.ShapeDtypeStruct((AUX, BW), F32),
        ),
        in_specs=[vm, hbm, hbm, hbm, vm, vm, pl.BlockSpec(memory_space=pltpu.SMEM)],
        out_specs=(vm, vm, vm, vm, vm),
        scratch_shapes=[
            v((SEQ, D), BF16),
            v((SEQ, D), BF16),
            v((D, BW), BF16),
            v((MW, D), BF16),
            v((SEQ, BW), BF16),
            v((SEQ, BW + HD), BF16),
            v((SEQ, MW), BF16),
            v((SEQ, MW), BF16),
            v((HEADS, SEQ, SEQ), BF16),
            v((SEQ, MW), BF16),
            v((HD, SEQ), F32),
            v((SEQ, HD), F32),
            v((SEQ, HD), F32),
            v((SEQ, HD), F32),
            v((SEQ, HD), F32),
            v((2, SEQ, HD), F32),
            v((CH, 8 * HS, BW + HD), BF16),
            v((CH, 2, 4 * HS, D), BF16),
            v((CH, 4 * HS, D), BF16),
            v((CH, 2, HS, HALF), BF16),
            v((CH, 2, HS, D), BF16),
            v((8, SEQ, 512), BF16),
            v((8, SEQ, 512), BF16),
            v((8, SEQ, MW), BF16),
            v((8, SEQ, BW), BF16),
            v((8, AUX, SEQ + HD), BF16),
            v((5, 8, 512), F32),
            v((8, 8, 512), F32),
            v((AUX, BW), F32),
            v((AUX, D), BF16),
            pltpu.SemaphoreType.DMA((3,)),
            pltpu.SemaphoreType.DMA((N_SEMS,)),
            pltpu.SemaphoreType.DMA((N_SEMS,)),
        ],
        compiler_params=pltpu.CompilerParams(
            collective_id=0, has_side_effects=True, vmem_limit_bytes=63 << 20
        ),
    )(
        section_inputs[0, 0, 0], grad_out[0, 0], in_weight[0], out_weight[0], gains, step_weight.T, decay_rate
    )
    ig, ing, outg, gaing, step, rates = pl.pallas_call(
        finish,
        out_shape=(
            jax.ShapeDtypeStruct((OWN, D), BF16),
            jax.ShapeDtypeStruct((512, BW), F32),
            jax.ShapeDtypeStruct((MW, 512), F32),
            jax.ShapeDtypeStruct((1, 64), F32),
            jax.ShapeDtypeStruct((HEADS, 256), F32),
            jax.ShapeDtypeStruct((1, HEADS), F32),
        ),
        in_specs=[far, far, far, vm, vm],
        out_specs=(far, far, far, vm, vm, vm),
        scratch_shapes=[
            v((OWN, D), BF16),
            v((512, BW), F32),
            v((MW, 512), F32),
            pltpu.SemaphoreType.DMA((2, 12)),
        ],
        compiler_params=pltpu.CompilerParams(vmem_limit_bytes=60 << 20),
    )(ig, ing, outg, gaing, aux)
    return (ig[None, None, None], ing[None], outg[None], gaing, step.T, rates[0])


def solution(mesh):
    return jax.shard_map(
        shards,
        mesh=mesh,
        in_specs=(
            P("dp", "pipe", None, "ts", None),
            P("dp", None, "ts", None),
            P("pipe", None, "ts"),
            P("pipe", "ts", None),
            P("pipe", None),
            P(None, "ts"),
            P("ts"),
        ),
        out_specs=(
            P("dp", "pipe", None, "ts", None),
            P("pipe", "dp", "ts"),
            P("pipe", "ts", "dp"),
            P("pipe", ("dp", "ts")),
            P(("dp", "pipe"), "ts"),
            P("ts"),
        ),
        check_vma=False,
    )
```
